32 devices in a mesh: shard: 4 (over y, x), replica: 8 (over z, core).
Axes of the slice: x: 2, y: 2, z: 4, core: 2. Of those that a mesh axis runs over, the one named last changes fastest.
Arguments:
- latents: bfloat16 [128, 256, 384], P(('shard', 'replica')), may hold values from -4 to 4
- conditioning: float32 [128, 384], P(('shard', 'replica')), may hold values from -2.5 to 2.5
- w_mod: bfloat16 [2, 384, 2304], P(None, 'shard'), may hold values from -0.3125 to 0.3125
- b_mod: bfloat16 [2, 2304], P(None, 'shard'), may hold values from -0.75 to 0.75
- w_qkv: bfloat16 [2, 384, 1152], P(None, 'shard'), may hold values from -0.3125 to 0.3125
- w_out: bfloat16 [2, 384, 384], P(None, 'shard'), may hold values from -1.25 to 1.25
- w_fc1: bfloat16 [2, 384, 1536], P(None, 'shard'), may hold values from -0.3125 to 0.3125
- w_fc2: bfloat16 [2, 1536, 384], P(None, 'shard'), may hold values from -0.15625 to 0.15625
- cotangent: bfloat16 [128, 256, 384], P(('shard', 'replica')), may hold values from -4 to 4
- live_counts: int32 [32], P(('shard', 'replica')), may hold values from 2 to 4, as said below
Outputs:
- output: bfloat16 [128, 256, 384], P(('shard', 'replica'))
- latents_grad: bfloat16 [128, 256, 384], P(('shard', 'replica'))
- conditioning_grad: float32 [128, 384], P(('shard', 'replica'))
- w_mod_grad: float32 [2, 384, 2304], P(None, 'shard')
- b_mod_grad: float32 [2, 2304], P(None, 'shard')
- w_qkv_grad: float32 [2, 384, 1152], P(None, 'shard')
- w_out_grad: float32 [2, 384, 384], P(None, 'shard')
- w_fc1_grad: float32 [2, 384, 1536], P(None, 'shard')
- w_fc2_grad: float32 [2, 1536, 384], P(None, 'shard')
The draws below stay inside these ranges and needn't reach their ends.
Inputs may be any that keep to these rules, and one draw needn't show every extreme that they name: `live_counts`: each device has at least half of its 4 slots live; in every draw some device has all 4 live and some other exactly 2.
All inputs are finite; a program needn't handle non-finite values.
Results may differ from the reference program's by a relative error of at most 0.02.
The reference program's roundings to bfloat16 on the way count: a program that leaves them out, or rounds other values in their place, can miss the bound.
Values may be sent and summed in bfloat16 or wider, within the bound.
No kernel may reach another device: no remote copies, remote signals or barrier semaphores. Data moves between devices by JAX's collectives and lax.ppermute only.
A program may use at most 128 MiB of HBM per device.

```python
import jax
import jax.numpy as jnp
from jax import lax

D = 384
HEADS = 6
HD = 64
FF = 1536
SEQ = 256
LAYERS = 2
LAT_DEV = 4
GROUPS = 32
SLOTS = 128


def draw_live_counts(key, part):
    key = jax.random.fold_in(key, 11)
    key_counts, key_ranking = jax.random.split(key)
    fewest = LAT_DEV - LAT_DEV // 2
    counts = jax.random.randint(key_counts, (GROUPS,), fewest, LAT_DEV + 1)
    ranking = jax.random.permutation(key_ranking, GROUPS)
    counts = counts.at[ranking[0]].set(LAT_DEV)
    counts = counts.at[ranking[1]].set(fewest)
    return counts.astype(jnp.int32)


def block_levels(rng, extent, shards, least, top_value):
    factor_of, own = 1.0, jax.random.fold_in(rng, 6)
    for dim, shards_of in shards:
        heights = jnp.exp(jax.random.uniform(jax.random.fold_in(own, dim), (shards_of,), jnp.float32, least / len(shards), top_value / len(shards)))
        factor_of = factor_of * jnp.repeat(heights, extent[dim] // shards_of).reshape([-1 if axis == dim else 1 for axis in range(len(extent))])
    return factor_of


def normal_values(own_key, dims, width, most, cuts=(), kind=jnp.bfloat16):
    factor_of = block_levels(own_key, dims, cuts, -0.22, 0.18) if cuts else 1.0
    entries = jax.random.normal(own_key, dims, jnp.float32) * width * factor_of
    return jnp.minimum(jnp.maximum(entries, -most), most).astype(kind)


def setup_inputs(seed: int = 0) -> dict:
    key_list = jax.random.split(jax.random.key(seed), 11)
    latents = normal_values(key_list[0], (SLOTS, SEQ, D), 1.0, 4.0, ((0, 32),))
    conditioning = normal_values(key_list[1], (SLOTS, D), 1.0, 2.5, ((0, 32),), jnp.float32)
    w_mod = normal_values(key_list[2], (LAYERS, D, 6 * D), D ** -0.5, 0.3125, ((1, 4),))
    b_mod = normal_values(key_list[3], (LAYERS, 6 * D), 0.3, 0.75, ((1, 4),))
    w_qkv = normal_values(key_list[4], (LAYERS, D, 3 * D), D ** -0.5, 0.3125, ((1, 4),))
    w_out = normal_values(key_list[5], (LAYERS, D, D), (D // 16) ** -0.5, 1.25, ((1, 4),))
    w_fc1 = normal_values(key_list[6], (LAYERS, D, FF), D ** -0.5, 0.3125, ((1, 4),))
    w_fc2 = normal_values(key_list[7], (LAYERS, FF, D), FF ** -0.5, 0.15625, ((1, 4),))
    cotangent = normal_values(key_list[8], (SLOTS, SEQ, D), 1.0, 4.0, ((0, 32),))
    live_counts = draw_live_counts(jax.random.fold_in(key_list[10], 71), 0)
    return {"latents": latents, "conditioning": conditioning, "w_mod": w_mod, "b_mod": b_mod, "w_qkv": w_qkv, "w_out": w_out, "w_fc1": w_fc1, "w_fc2": w_fc2, "cotangent": cotangent, "live_counts": live_counts}


EPS = 1e-06

@jax.custom_vjp
def low(v):
    return lax.optimization_barrier(v.astype(jnp.bfloat16)).astype(jnp.float32)

@jax.custom_vjp
def low_back(v):
    return v

def low_keep(v):
    return (low(v), None)

def low_pass(kept, grad):
    return (grad,)

def back_keep(v):
    return (v, None)

def back_low(kept, grad):
    return (low(grad),)
low.defvjp(low_keep, low_pass)
low_back.defvjp(back_keep, back_low)

def product(left, right):
    return jnp.matmul(left, right, precision=lax.Precision.HIGHEST)

def layer_norm(values):
    centered = values - lax.optimization_barrier(jnp.mean(values, -1, keepdims=True))
    variance = lax.optimization_barrier(jnp.mean(centered * centered, -1, keepdims=True))
    return centered * lax.rsqrt(variance + EPS)

def modulate(inputs, shift_by, scale_by):
    return layer_norm(inputs) * (1.0 + scale_by) + shift_by

def gelu_tanh(values):
    return jax.nn.gelu(values, approximate=True)

def attend(trio):
    queries, keys_all, values_all = trio
    scores = low_back(jnp.einsum('qhd,khd->hqk', queries, keys_all, precision=lax.Precision.HIGHEST)) * HD ** (-0.5)
    weights = low(jax.nn.softmax(scores, axis=-1))
    return jnp.einsum('hqk,khd->qhd', weights, values_all, precision=lax.Precision.HIGHEST)

def run_layer(state, silu_low, params):
    w_mod, b_mod, w_qkv, w_out, w_fc1, w_fc2 = params
    modulation = low_back(product(silu_low, w_mod)) + b_mod
    parts = [piece[:, None, :] for piece in jnp.split(modulation, 6, axis=-1)]
    shift_a, scale_a, gate_a, shift_f, scale_f, gate_f = parts
    normed = low(modulate(state, shift_a, scale_a))
    packed = low(low_back(product(normed, w_qkv)))
    count = state.shape[0]
    heads = packed.reshape(count, SEQ, 3, HEADS, HD)
    mixed = lax.map(jax.checkpoint(attend), (heads[:, :, 0], heads[:, :, 1], heads[:, :, 2]))
    mixed = low(low_back(mixed.reshape(count, SEQ, D)))
    middle = state + gate_a * low_back(product(mixed, w_out))
    normed_mid = low(modulate(middle, shift_f, scale_f))
    activ = low(gelu_tanh(low_back(product(normed_mid, w_fc1))))
    return middle + gate_f * low_back(product(activ, w_fc2))

def reference(latents, conditioning, w_mod, b_mod, w_qkv, w_out, w_fc1, w_fc2, cotangent, live_counts):
    params = tuple((array.astype(jnp.float32) for array in (w_mod, b_mod, w_qkv, w_out, w_fc1, w_fc2)))
    groups = live_counts.shape[0]
    lat_in = latents.reshape(groups, LAT_DEV, SEQ, D)
    cond_in = conditioning.reshape(groups, LAT_DEV, D)
    cot_in = cotangent.reshape(groups, LAT_DEV, SEQ, D)

    def group_step(totals, group_in):
        lat_now, cond_now, cot_now, count_now = group_in
        live_rows = (jnp.arange(LAT_DEV).astype(jnp.int32) < count_now.astype(jnp.int32))[:, None, None]

        def forward(state, cond_vals, weights):
            silu_low = low(jax.nn.silu(cond_vals))
            for layer_at in range(LAYERS):
                state = run_layer(state, silu_low, tuple((array[layer_at] for array in weights)))
            return jnp.where(live_rows, state, jnp.zeros_like(state))
        result, pullback = jax.vjp(forward, lat_now.astype(jnp.float32), cond_now, params)
        d_lat, d_cond, d_weights = pullback(cot_now.astype(jnp.float32))
        totals = tuple((first + second for first, second in zip(totals, d_weights)))
        return (totals, (result.astype(jnp.bfloat16), d_lat.astype(jnp.bfloat16), d_cond))
    start = tuple((jnp.zeros_like(array) for array in params))
    totals, (outputs, lat_grads, cond_grads) = lax.scan(group_step, start, (lat_in, cond_in, cot_in, live_counts))
    return (outputs.reshape(groups * LAT_DEV, SEQ, D), lat_grads.reshape(groups * LAT_DEV, SEQ, D), cond_grads.reshape(groups * LAT_DEV, D), totals[0], totals[1], totals[2], totals[3], totals[4], totals[5])
```

```python
import functools
import math

import jax
import jax.numpy as jnp
from jax import lax
from jax.experimental import pallas as pl
from jax.experimental.pallas import tpu as pltpu
from jax.sharding import PartitionSpec as P

D = 384
HEADS = 6
HD = 64
FF = 1536
SEQ = 256
LAYERS = 2
EPS = 1e-06
SCALE = HD**-0.5
HALF = FF // 2

F32 = jnp.float32
BF16 = jnp.bfloat16
VMEM_LIMIT = 56 * 1024 * 1024


def dot_nn(left, right):
    return jnp.dot(left, right, preferred_element_type=F32)


def dot_nt(left, right):
    return lax.dot_general(left, right, (((1,), (1,)), ((), ())), preferred_element_type=F32)


def as_columns(row):
    half = jnp.broadcast_to(row, (128, D)).T
    return jnp.concatenate([half, half], axis=1)


def token_sum(values):
    folded = values[:, :128] + values[:, 128:]
    return jnp.sum(folded.T, axis=0, keepdims=True)


def layer_norm(values):
    centered = values - jnp.mean(values, axis=0, keepdims=True)
    variance = jnp.mean(centered * centered, axis=0, keepdims=True)
    rstd = lax.rsqrt(variance + EPS)
    return centered * rstd, rstd


def layer_norm_pull(d_out, normal, rstd, scale_col):
    d_normal = d_out * (1.0 + scale_col)
    first = jnp.mean(d_normal, axis=0, keepdims=True)
    second = jnp.mean(d_normal * normal, axis=0, keepdims=True)
    return rstd * (d_normal - first - normal * second)


def lanes(index):
    return pl.ds(pl.multiple_of(index * SEQ, SEQ), SEQ)


def mod_row(mod_ref, latent, layer, part):
    start = layer * 6 * D + part * D
    return mod_ref[pl.ds(latent, 1), start : start + D]


def attend_forward(group, x_of, mod_ref, first, layer, w_t, normed, qkv, mixed, lse, proj, x_mid):
    for i in range(group):
        normal, _ = layer_norm(x_of(i))
        shift = as_columns(mod_row(mod_ref, first + i, layer, 0))
        scale = as_columns(mod_row(mod_ref, first + i, layer, 1))
        normed[:, i * SEQ : (i + 1) * SEQ] = (normal * (1.0 + scale) + shift).astype(BF16)
    for part in range(3):
        rows = slice(part * D, (part + 1) * D)
        packed = dot_nn(w_t[rows, :], normed[...])
        if part == 0:
            qkv[rows, :] = packed.astype(BF16) * jnp.asarray(SCALE, BF16)
        else:
            qkv[rows, :] = packed.astype(BF16)

    def head_step(step, carry):
        cols = lanes(step // (HEADS // 2))
        pair = step % (HEADS // 2)
        for side in range(2):
            head = pair * 2 + side
            row = pl.multiple_of(head * HD, HD)
            q_t = qkv[pl.ds(row, HD), cols]
            k_t = qkv[pl.ds(row + D, HD), cols]
            v_t = qkv[pl.ds(row + 2 * D, HD), cols]
            scores = dot_nn(k_t.T, q_t)
            highest = jnp.max(scores, axis=0, keepdims=True)
            probs = jnp.exp(scores - highest)
            total = jnp.sum(probs, axis=0, keepdims=True)
            out = dot_nn(v_t, probs.astype(BF16)) * (1.0 / total)
            mixed[pl.ds(row, HD), cols] = out.astype(BF16)
            lse[pl.ds(head, 1), cols] = highest + jnp.log(total)
        return carry

    lax.fori_loop(0, group * (HEADS // 2), head_step, 0, unroll=HEADS // 2)
    projected = dot_nn(w_t[3 * D :, :], mixed[...])
    proj[...] = projected.astype(BF16)
    for i in range(group):
        gate = as_columns(mod_row(mod_ref, first + i, layer, 2))
        cols = slice(i * SEQ, (i + 1) * SEQ)
        x_mid[:, cols] = x_of(i) + gate * projected[:, cols]


def feed_forward(group, mod_ref, first, layer, w1_t, w2_t, x_mid, normed_mid, act, slope, lift, x_out):
    for i in range(group):
        cols = slice(i * SEQ, (i + 1) * SEQ)
        normal, _ = layer_norm(x_mid[:, cols])
        shift = as_columns(mod_row(mod_ref, first + i, layer, 3))
        scale = as_columns(mod_row(mod_ref, first + i, layer, 4))
        normed_mid[:, cols] = (normal * (1.0 + scale) + shift).astype(BF16)
    chunk = 384

    def hidden_step(step, carry):
        rows = pl.ds(pl.multiple_of(step * chunk, chunk), chunk)
        hidden = dot_nn(w1_t[rows, :], normed_mid[...])
        root = math.sqrt(2.0 / math.pi)
        square = hidden * hidden
        bent = jnp.tanh(hidden * (root + (root * 0.044715) * square))
        half = 0.5 + 0.5 * bent
        act[rows, :] = (hidden * half).astype(BF16)
        inner = root + (3.0 * root * 0.044715) * square
        slope[rows, :] = (half + hidden * inner * (half * (1.0 - bent))).astype(BF16)
        return carry

    lax.fori_loop(0, FF // chunk, hidden_step, 0, unroll=True)
    lifted = dot_nn(w2_t[...], act[...])
    lift[...] = lifted.astype(BF16)
    for i in range(group):
        gate = as_columns(mod_row(mod_ref, first + i, layer, 5))
        cols = slice(i * SEQ, (i + 1) * SEQ)
        x_out[:, cols] = x_mid[:, cols] + gate * lifted[:, cols]


def feed_backward(
    group, mod_ref, first, layer, w1, w2, grad, x_mid, normed_mid, act, slope, lift,
    d_lift, d_hidden, g1, g2, d_mod, base, grad_mid,
):
    for i in range(group):
        cols = slice(i * SEQ, (i + 1) * SEQ)
        gate = as_columns(mod_row(mod_ref, first + i, layer, 5))
        grad_now = grad[:, cols]
        d_lift[:, cols] = (grad_now * gate).astype(BF16)
        d_mod[pl.ds(first + i, 1), base + 2 * D : base + 3 * D] = token_sum(
            grad_now * lift[:, cols].astype(F32)
        )
    chunk = 512

    def hidden_step(step, carry):
        rows = pl.ds(pl.multiple_of(step * chunk, chunk), chunk)
        d_act = dot_nn(w2[rows, :], d_lift[...])
        d_hid = (d_act * slope[rows, :].astype(F32)).astype(BF16)
        d_hidden[rows, :] = d_hid
        g2[rows, :] += dot_nt(act[rows, :], d_lift[...])
        g1[:, rows] += dot_nt(normed_mid[...], d_hid)
        return carry

    lax.fori_loop(0, FF // chunk, hidden_step, 0, unroll=True)
    d_normed = dot_nn(w1[...], d_hidden[...])
    for i in range(group):
        cols = slice(i * SEQ, (i + 1) * SEQ)
        d_now = d_normed[:, cols]
        normal, rstd = layer_norm(x_mid[:, cols])
        scale = as_columns(mod_row(mod_ref, first + i, layer, 4))
        row = pl.ds(first + i, 1)
        d_mod[row, base : base + D] = token_sum(d_now)
        d_mod[row, base + D : base + 2 * D] = token_sum(d_now * normal)
        grad_mid[:, cols] = grad[:, cols] + layer_norm_pull(d_now, normal, rstd, scale)


def attend_backward(
    group, x_of, mod_ref, first, layer, w_attn, grad_mid, normed, qkv, mixed, lse, proj,
    d_proj, d_mixed, d_qkv, g_attn, d_mod, base, emit,
):
    for i in range(group):
        cols = slice(i * SEQ, (i + 1) * SEQ)
        gate = as_columns(mod_row(mod_ref, first + i, layer, 2))
        grad_now = grad_mid[:, cols]
        d_proj[:, cols] = (grad_now * gate).astype(BF16)
        d_mod[pl.ds(first + i, 1), base + 2 * D : base + 3 * D] = token_sum(
            grad_now * proj[:, cols].astype(F32)
        )
    d_mixed[...] = dot_nn(w_attn[:, 3 * D :], d_proj[...]).astype(BF16)
    g_attn[:, 3 * D :] += dot_nt(mixed[...], d_proj[...])

    def head_step(step, carry):
        cols = lanes(step // (HEADS // 2))
        pair = step % (HEADS // 2)
        for side in range(2):
            head = pair * 2 + side
            row = pl.multiple_of(head * HD, HD)
            q_t = qkv[pl.ds(row, HD), cols]
            k_t = qkv[pl.ds(row + D, HD), cols]
            v_t = qkv[pl.ds(row + 2 * D, HD), cols]
            d_out = d_mixed[pl.ds(row, HD), cols]
            scores = dot_nn(k_t.T, q_t)
            probs = jnp.exp(scores - lse[pl.ds(head, 1), cols])
            d_probs = dot_nn(v_t.T, d_out)
            delta = jnp.sum(probs * d_probs, axis=0, keepdims=True)
            d_scores = (probs * (d_probs - delta)).astype(BF16)
            d_qkv[pl.ds(row, HD), cols] = (dot_nn(k_t, d_scores) * SCALE).astype(BF16)
            d_qkv[pl.ds(row + D, HD), cols] = dot_nt(q_t, d_scores).astype(BF16)
            d_qkv[pl.ds(row + 2 * D, HD), cols] = dot_nt(d_out, probs.astype(BF16)).astype(BF16)
        return carry

    lax.fori_loop(0, group * (HEADS // 2), head_step, 0, unroll=HEADS // 2)
    for part in range(3):
        rows = slice(part * D, (part + 1) * D)
        g_attn[:, rows] += dot_nt(normed[...], d_qkv[rows, :])
    d_normed = dot_nn(w_attn[:, : 3 * D], d_qkv[...])
    for i in range(group):
        cols = slice(i * SEQ, (i + 1) * SEQ)
        d_now = d_normed[:, cols]
        normal, rstd = layer_norm(x_of(i))
        scale = as_columns(mod_row(mod_ref, first + i, layer, 1))
        row = pl.ds(first + i, 1)
        d_mod[row, base : base + D] = token_sum(d_now)
        d_mod[row, base + D : base + 2 * D] = token_sum(d_now * normal)
        emit(i, grad_mid[:, cols] + layer_norm_pull(d_now, normal, rstd, scale))


def place_rows(shards, me, core, own, near, far, pack, target):
    rows = D // shards
    target[pl.ds(pl.multiple_of(me * rows, rows), rows), :] = own[pack]
    for k in range(1, shards):
        at = pl.ds(pl.multiple_of((me ^ k) * rows, rows), rows)
        target[at, pl.ds(pl.multiple_of(core * HALF, HALF), HALF)] = near[k - 1][pack]
        target[at, pl.ds(pl.multiple_of((1 - core) * HALF, HALF), HALF)] = far[k - 1][pack]


def unfold_second(shards, packed, natural):
    rows = D // shards
    for s in range(shards):
        for q in range(FF // D):
            start = s * (FF // shards) + q * rows
            natural[start : start + rows, :] = packed[
                s * rows : (s + 1) * rows, q * D : (q + 1) * D
            ]


def emit_grads(shards, me, core, g_attn, g1, g2, keep, send):
    rows = D // shards
    packs = [array for array in (g_attn, g1) if array is not None]
    for k in range(shards):
        owner = me ^ k
        start = pl.multiple_of(owner * rows, rows)
        for target, side in ((keep, core), (send, 1 - core)):
            cols = pl.ds(pl.multiple_of(side * HALF, HALF), HALF)
            for at, array in enumerate(packs):
                target[k, at] = array[pl.ds(start, rows), cols].astype(BF16)
            if g2 is not None:
                for q in range(HALF // D):
                    begin = owner * (FF // shards) + (side * (HALF // D) + q) * rows
                    target[k, len(packs), :, q * D : (q + 1) * D] = g2[
                        pl.ds(pl.multiple_of(begin, rows), rows), :
                    ].astype(BF16)


def whole():
    return None


def filled(specs, arrays):
    return [
        pl.BlockSpec(array.shape, lambda *_, dims=array.ndim: (0,) * dims) if spec is None else spec
        for spec, array in zip(specs, arrays, strict=True)
    ]


def scalars():
    return pl.BlockSpec(memory_space=pltpu.SMEM)


def by_step(rows, group):
    return pl.BlockSpec((rows, group * SEQ), lambda step: (0, step))


def by_latent(group):
    return pl.BlockSpec((group, SEQ, D), lambda step: (step, 0, 0))


def shape_of(shape, dtype):
    return jax.ShapeDtypeStruct(shape, dtype)


def cost(flops, nbytes):
    return pl.CostEstimate(flops=int(flops), bytes_accessed=int(nbytes), transcendentals=0)


def run_kernel(body, name, steps, in_specs, out_specs, out_shape, scratch, flops, args):
    return pl.pallas_call(
        body,
        name=name,
        grid=(steps,),
        in_specs=filled(in_specs, args),
        out_specs=filled(out_specs, out_shape),
        out_shape=out_shape,
        scratch_shapes=scratch,
        cost_estimate=cost(8 * flops, 8 << 20),
        compiler_params=pltpu.CompilerParams(
            dimension_semantics=("arbitrary",), vmem_limit_bytes=VMEM_LIMIT
        ),
    )(*args)


def modulation_partials(shards, scal, cond_pieces, w_mod, b_mod):
    count = cond_pieces[0].shape[0]
    total = shards * count
    rows = D // shards
    wide = 6 * D

    def body(scal_ref, *refs):
        conds = refs[:shards]
        w_ref, b_ref = refs[shards : shards + 2]
        outs = refs[shards + 2 : 2 * shards + 2]
        table, turned = refs[2 * shards + 2 :]
        me = scal_ref[0]
        table[...] = jnp.zeros_like(table)
        for k in range(shards):
            table[k * count : (k + 1) * count, :] = conds[k][...]
        values = table[...]
        turned[...] = (values / (1.0 + jnp.exp(-values))).T
        mine = turned[pl.ds(pl.multiple_of(me * rows, rows), rows), :].T[:total, :].astype(BF16)
        owner = lax.broadcasted_iota(jnp.int32, (1, wide), 1) // (wide // shards)
        for layer in range(LAYERS):
            bias = jnp.concatenate([b_ref[layer : layer + 1, :].astype(F32)] * shards, axis=1)
            part = dot_nn(mine, w_ref[layer]) + jnp.where(owner == me, bias, 0.0)
            for k in range(shards):
                outs[k][:, layer * wide : (layer + 1) * wide] = part[k * count : (k + 1) * count, :]

    return small_kernel(
        body, "modulation_parts", [shape_of((count, LAYERS * wide), F32)] * shards,
        [pltpu.VMEM((128, D), F32), pltpu.VMEM((D, 128), F32)],
        (scal, *cond_pieces, w_mod, b_mod), 1,
    )


def first_attention(shards, group, scal, latents, mods, own, near, far):
    count = latents.shape[0]
    tokens = count * SEQ
    pieces = 2 * (shards - 1)

    def body(scal_ref, lat_ref, *refs):
        mod_refs = refs[:shards]
        own_ref = refs[shards]
        near_refs = refs[shards + 1 : shards + 1 + pieces // 2]
        far_refs = refs[shards + 1 + pieces // 2 : shards + 1 + pieces]
        mod, w_nat, normed, qkv, mixed, lse, proj, x_mid, w_t = refs[shards + 1 + pieces :]
        step = pl.program_id(0)

        @pl.when(step == 0)
        def _():
            total = mod_refs[0][...]
            for ref in mod_refs[1:]:
                total = total + ref[...]
            mod[...] = total
            place_rows(shards, scal_ref[0], scal_ref[1], own_ref, near_refs, far_refs, 0, w_nat)
            w_t[...] = w_nat[...].T

        def x_of(i):
            return lat_ref[i].astype(F32).T

        attend_forward(
            group, x_of, mod, step * group, 0, w_t, normed, qkv, mixed, lse, proj, x_mid
        )

    return run_kernel(
        body, "attention_0", count // group,
        [scalars(), by_latent(group)] + [whole()] * (shards + 1 + pieces),
        [whole(), whole()]
        + [by_step(r, group) for r in (D, 3 * D, D, HEADS, D, D)],
        [
            shape_of((count, LAYERS * 6 * D), F32),
            shape_of((D, FF), BF16),
            shape_of((D, tokens), BF16),
            shape_of((3 * D, tokens), BF16),
            shape_of((D, tokens), BF16),
            shape_of((HEADS, tokens), F32),
            shape_of((D, tokens), BF16),
            shape_of((D, tokens), F32),
        ],
        [pltpu.VMEM((FF, D), BF16)],
        2 * tokens * (4 * D * D + 2 * SEQ * D),
        (scal, latents, *mods, own, *near, *far),
    )


def first_feed(shards, group, scal, mod, own, near, far, x_mid):
    tokens = x_mid.shape[1]
    count = tokens // SEQ
    pieces = 2 * (shards - 1)

    def body(scal_ref, mod_ref, own_ref, *refs):
        near_refs = refs[: pieces // 2]
        far_refs = refs[pieces // 2 : pieces]
        x_mid_ref = refs[pieces]
        w1, w2, normed_mid, act, slope, lift, x_out, packed, w1_t, w2_t = refs[pieces + 1 :]
        step = pl.program_id(0)

        @pl.when(step == 0)
        def _():
            me, core = scal_ref[0], scal_ref[1]
            place_rows(shards, me, core, own_ref, near_refs, far_refs, 0, w1)
            place_rows(shards, me, core, own_ref, near_refs, far_refs, 1, packed)
            unfold_second(shards, packed, w2)
            w1_t[...] = w1[...].T
            w2_t[...] = w2[...].T

        feed_forward(
            group, mod_ref, step * group, 0, w1_t, w2_t, x_mid_ref, normed_mid, act, slope, lift,
            x_out,
        )

    return run_kernel(
        body, "feed_0", count // group,
        [scalars(), whole(), whole()] + [whole()] * pieces + [by_step(D, group)],
        [whole(), whole()] + [by_step(r, group) for r in (D, FF, FF, D, D)],
        [
            shape_of((D, FF), BF16),
            shape_of((FF, D), BF16),
            shape_of((D, tokens), BF16),
            shape_of((FF, tokens), BF16),
            shape_of((FF, tokens), BF16),
            shape_of((D, tokens), BF16),
            shape_of((D, tokens), F32),
        ],
        [pltpu.VMEM((D, FF), BF16), pltpu.VMEM((FF, D), BF16), pltpu.VMEM((D, FF), BF16)],
        4 * tokens * D * FF,
        (scal, mod, own, *near, *far, x_mid),
    )


def last_layer(shards, group, scal, mod, own, near, far, x_in, cotangent):
    tokens = x_in.shape[1]
    count = tokens // SEQ
    steps = count // group
    pieces = 4 * (shards - 1)
    layer = LAYERS - 1
    rows = D // shards
    wide = group * SEQ

    def body(scal_ref, mod_ref, own_ref, *refs):
        near_refs = refs[: pieces // 2]
        far_refs = refs[pieces // 2 : pieces]
        x_ref, cot_ref = refs[pieces : pieces + 2]
        (
            output, grad_mid, d_mod, keep, send, w_attn, normed, qkv, mixed, lse, proj,
        ) = refs[pieces + 2 : pieces + 13]
        (
            w1, w2, attn_t, w1_t, w2_t, x_mid, normed_mid, act, slope, lift, x_out, grad,
            d_lift, d_hidden, g1, g2,
        ) = refs[pieces + 13 :]
        step = pl.program_id(0)
        me, core, live = scal_ref[0], scal_ref[1], scal_ref[2]
        first = step * group

        @pl.when(step == 0)
        def _():
            near_1, near_2 = near_refs[: shards - 1], near_refs[shards - 1 :]
            far_1, far_2 = far_refs[: shards - 1], far_refs[shards - 1 :]
            place_rows(shards, me, core, own_ref.at[:1], near_1, far_1, 0, w_attn)
            place_rows(shards, me, core, own_ref.at[1:], near_2, far_2, 1, w1)
            unfold_second(shards, w1, w2)
            place_rows(shards, me, core, own_ref.at[1:], near_2, far_2, 0, w1)
            attn_t[...] = w_attn[...].T
            w1_t[...] = w1[...].T
            w2_t[...] = w2[...].T
            g1[...] = jnp.zeros_like(g1)
            g2[...] = jnp.zeros_like(g2)

        def x_of(i):
            return x_ref[:, i * SEQ : (i + 1) * SEQ]

        attend_forward(
            group, x_of, mod_ref, first, layer, attn_t, normed, qkv, mixed, lse, proj, x_mid
        )
        feed_forward(
            group, mod_ref, first, layer, w1_t, w2_t, x_mid, normed_mid, act, slope, lift, x_out
        )
        for i in range(group):
            cols = slice(i * SEQ, (i + 1) * SEQ)
            is_live = first + i < live
            output[i] = jnp.where(is_live, x_out[:, cols].T, 0.0).astype(BF16)
            grad[:, cols] = jnp.where(is_live, cot_ref[i].astype(F32).T, 0.0)
        feed_backward(
            group, mod_ref, first, layer, w1, w2, grad, x_mid, normed_mid, act, slope, lift,
            d_lift, d_hidden, g1, g2, d_mod, 0, grad_mid,
        )

        @pl.when(step == steps - 1)
        def _():
            emit_grads(shards, me, core, None, g1, g2, keep, send)

    def vm(rows, cols, dtype):
        return pltpu.VMEM((rows, cols), dtype)

    return run_kernel(
        body, "layer_1", steps,
        [scalars(), whole(), whole()] + [whole()] * pieces + [by_step(D, group), by_latent(group)],
        [by_latent(group), by_step(D, group), whole(), whole(), whole(), whole()]
        + [by_step(r, group) for r in (D, 3 * D, D, HEADS, D)],
        [
            shape_of((count, SEQ, D), BF16),
            shape_of((D, tokens), F32),
            shape_of((count, 3 * D), F32),
            shape_of((shards, 2, rows, HALF), BF16),
            shape_of((shards, 2, rows, HALF), BF16),
            shape_of((D, FF), BF16),
            shape_of((D, tokens), BF16),
            shape_of((3 * D, tokens), BF16),
            shape_of((D, tokens), BF16),
            shape_of((HEADS, tokens), F32),
            shape_of((D, tokens), BF16),
        ],
        [
            vm(D, FF, BF16), vm(FF, D, BF16), vm(FF, D, BF16), vm(FF, D, BF16), vm(D, FF, BF16),
            vm(D, wide, F32), vm(D, wide, BF16), vm(FF, wide, BF16), vm(FF, wide, BF16),
            vm(D, wide, BF16), vm(D, wide, F32), vm(D, wide, F32), vm(D, wide, BF16),
            vm(FF, wide, BF16), vm(D, FF, F32), vm(FF, D, F32),
        ],
        4 * tokens * (4 * D * D + 4 * D * FF + 2 * SEQ * D),
        (scal, mod, own, *near, *far, x_in, cotangent),
    )


def first_feed_back(shards, group, scal, mod, w1, w2, grad, x_mid, normed_mid, act, slope, lift):
    tokens = grad.shape[1]
    count = tokens // SEQ
    steps = count // group
    rows = D // shards
    wide = group * SEQ

    def body(
        scal_ref, mod_ref, w1_ref, w2_ref, grad_ref, x_ref, nm_ref, act_ref, slope_ref, lift_ref,
        grad_mid, d_mod, keep, send, d_lift, d_hidden, g1, g2,
    ):
        step = pl.program_id(0)

        @pl.when(step == 0)
        def _():
            g1[...] = jnp.zeros_like(g1)
            g2[...] = jnp.zeros_like(g2)

        feed_backward(
            group, mod_ref, step * group, 0, w1_ref, w2_ref, grad_ref, x_ref, nm_ref, act_ref,
            slope_ref, lift_ref, d_lift, d_hidden, g1, g2, d_mod, 0, grad_mid,
        )

        @pl.when(step == steps - 1)
        def _():
            emit_grads(shards, scal_ref[0], scal_ref[1], None, g1, g2, keep, send)

    return run_kernel(
        body, "feed_back_0", steps,
        [scalars(), whole(), whole(), whole()]
        + [by_step(r, group) for r in (D, D, D, FF, FF, D)],
        [by_step(D, group), whole(), whole(), whole()],
        [
            shape_of((D, tokens), F32),
            shape_of((count, 3 * D), F32),
            shape_of((shards, 2, rows, HALF), BF16),
            shape_of((shards, 2, rows, HALF), BF16),
        ],
        [
            pltpu.VMEM((D, wide), BF16), pltpu.VMEM((FF, wide), BF16),
            pltpu.VMEM((D, FF), F32), pltpu.VMEM((FF, D), F32),
        ],
        8 * tokens * D * FF,
        (scal, mod, w1, w2, grad, x_mid, normed_mid, act, slope, lift),
    )


def attention_back(
    shards, group, layer, scal, mod, w_attn, grad_mid, x_in, normed, qkv, mixed, lse, proj
):
    tokens = grad_mid.shape[1]
    count = tokens // SEQ
    steps = count // group
    rows = D // shards
    wide = group * SEQ

    def body(
        scal_ref, mod_ref, w_ref, grad_ref, x_ref, normed_ref, qkv_ref, mixed_ref, lse_ref,
        proj_ref, grad_out, d_mod, keep, send, d_proj, d_mixed, d_qkv, g_attn,
    ):
        step = pl.program_id(0)

        @pl.when(step == 0)
        def _():
            g_attn[...] = jnp.zeros_like(g_attn)

        def x_of(i):
            if layer == 0:
                return x_ref[i].astype(F32).T
            return x_ref[:, i * SEQ : (i + 1) * SEQ]

        def emit(i, values):
            if layer == 0:
                grad_out[i] = values.T.astype(BF16)
            else:
                grad_out[:, i * SEQ : (i + 1) * SEQ] = values

        attend_backward(
            group, x_of, mod_ref, step * group, layer, w_ref, grad_ref, normed_ref, qkv_ref,
            mixed_ref, lse_ref, proj_ref, d_proj, d_mixed, d_qkv, g_attn, d_mod, 0, emit,
        )

        @pl.when(step == steps - 1)
        def _():
            emit_grads(shards, scal_ref[0], scal_ref[1], g_attn, None, None, keep, send)

    io_spec = by_latent(group) if layer == 0 else by_step(D, group)
    out_form = shape_of((count, SEQ, D), BF16) if layer == 0 else shape_of((D, tokens), F32)
    return run_kernel(
        body, f"attention_back_{layer}", steps,
        [scalars(), whole(), whole(), by_step(D, group), io_spec]
        + [by_step(r, group) for r in (D, 3 * D, D, HEADS, D)],
        [io_spec, whole(), whole(), whole()],
        [
            out_form,
            shape_of((count, 3 * D), F32),
            shape_of((shards, 1, rows, HALF), BF16),
            shape_of((shards, 1, rows, HALF), BF16),
        ],
        [
            pltpu.VMEM((D, wide), BF16), pltpu.VMEM((D, wide), BF16),
            pltpu.VMEM((3 * D, wide), BF16), pltpu.VMEM((D, FF), F32),
        ],
        4 * tokens * (4 * D * D + 3 * SEQ * D),
        (scal, mod, w_attn, grad_mid, x_in, normed, qkv, mixed, lse, proj),
    )


BLOCKS = 2


def small_kernel(body, name, outs, scratch, args, smem=0):
    specs = [scalars()] * smem + [whole()] * (len(args) - smem)
    return pl.pallas_call(
        body,
        name=name,
        grid=(1,),
        in_specs=filled(specs, args),
        out_specs=filled([whole()] * len(outs), outs),
        out_shape=outs,
        scratch_shapes=scratch,
        cost_estimate=cost(1, 1),
        compiler_params=pltpu.CompilerParams(vmem_limit_bytes=VMEM_LIMIT),
    )(*args)


def silu(values):
    return values / (1.0 + jnp.exp(-values))


def start_messages(shards, name, keep, arrived, d_mod, conditioning):
    packs, rows = keep.shape[1:3]
    count = d_mod.shape[0]
    tail = BLOCKS * count
    tail = -(-tail // 16) * 16

    def body(keep_ref, arrived_ref, d_ref, *refs):
        cond_ref = refs[0] if conditioning is not None else None
        outs, table = refs[len(refs) - shards - 1 : -1], refs[-1]
        table[...] = jnp.zeros_like(table)
        table[:count, :] = d_ref[:, :HALF]
        table[count : 2 * count, : 3 * D - HALF] = d_ref[:, HALF:]
        if cond_ref is not None:
            table[count : 2 * count, 3 * D - HALF :] = silu(cond_ref[...])
        low = table[...].astype(BF16)
        for k in range(shards):
            for j in range(packs):
                total = keep_ref[k, j].astype(F32) + arrived_ref[k, j].astype(F32)
                outs[k][j * rows : (j + 1) * rows, :] = total.astype(BF16)
            outs[k][packs * rows :, :] = low

    args = (keep, arrived, d_mod) + (() if conditioning is None else (conditioning,))
    return small_kernel(
        body, name, [shape_of((packs * rows + tail, HALF), BF16)] * shards,
        [pltpu.VMEM((tail, HALF), F32)], args,
    )


def shard_sums(shards, name, count, members, scal, messages):
    rows = D // shards
    span = shards * count
    all_packs = sum(packs for packs, _ in members)
    all_parts = sum(parts for _, parts in members)

    def body(scal_ref, *refs):
        keep, send, joined, total, table = refs[shards * len(members) :]
        odd = (scal_ref[3] // 2) % 2
        first_pack, first_part = 0, 0
        for m, (packs, parts) in enumerate(members):
            ins = refs[shards * m : shards * (m + 1)]
            value = ins[0][: packs * rows, :].astype(F32)
            for k in range(1, shards):
                value = value + ins[k][: packs * rows, :].astype(F32)
            total[first_pack * rows : (first_pack + packs) * rows, :] = value
            for k in range(shards):
                extra = ins[k][packs * rows :, :].astype(F32)
                for b in range(parts):
                    at = (first_part + b) * span + k * count
                    first = (b // 2) * count
                    table[at : at + count, :] = extra[
                        first : first + count, (b % 2) * D : (b % 2 + 1) * D
                    ]
            first_pack += packs
            first_part += parts
        keep[...] = total[:, pl.ds(pl.multiple_of(odd * D, D), D)].astype(BF16)
        send[...] = total[:, pl.ds(pl.multiple_of((1 - odd) * D, D), D)].astype(BF16)
        joined[...] = table[...].astype(BF16)

    return small_kernel(
        body, name,
        [
            shape_of((all_packs * rows, D), BF16), shape_of((all_packs * rows, D), BF16),
            shape_of((all_parts * span, D), BF16),
        ],
        [pltpu.VMEM((all_packs * rows, HALF), F32), pltpu.VMEM((all_parts * span, D), F32)],
        (scal, *[message for phase in messages for message in phase]), 1,
    )


def pair_sums(name, keep, arrived, joined):
    size, extra = keep.shape[0], joined.shape[0]

    def body(a, b, c, out):
        out[:size, :] = (a[...].astype(F32) + b[...].astype(F32)).astype(BF16)
        out[size:, :] = c[...]

    return small_kernel(
        body, name, [shape_of((size + extra, D), BF16)], [], (keep, arrived, joined)
    )[0]


def chip_sums(name, size, ours, theirs):
    extra = ours.shape[0] - size

    def body(a, b, out):
        total = a[:size, :].astype(F32) + b[:size, :].astype(F32)
        out[:size, :] = total.astype(BF16)
        out[size : size + extra, :] = a[size:, :]
        out[size + extra :, :] = b[size:, :]

    return small_kernel(
        body, name, [shape_of((size + 2 * extra, D), BF16)], [], (ours, theirs)
    )[0]


def silu_grad_parts(shards, count, w_mod, places, joined):
    rows = D // shards
    span = shards * count

    def body(*refs):
        w_ref = refs[len(joined)]
        outs = refs[len(joined) + 1 :]
        total = None
        for (layer, half), (at, first) in places.items():
            for b in range(3):
                part = dot_nt(
                    refs[at][(first + b) * span : (first + b + 1) * span, :],
                    w_ref[layer, :, (3 * half + b) * D : (3 * half + b + 1) * D],
                )
                total = part if total is None else total + part
        for k in range(shards):
            outs[k][...] = total[k * count : (k + 1) * count, :]

    return small_kernel(
        body, "silu_grad_parts", [shape_of((count, rows), F32)] * shards, [], (*joined, w_mod),
    )


def finish_feeds(shards, scal, feeds):
    rows = D // shards

    def body(scal_ref, *refs):
        g_one, g_two = refs[4 * LAYERS :]
        core, odd = scal_ref[1], (scal_ref[3] // 2) % 2
        for layer, (pack, _) in enumerate(feeds):
            for at in range(4):
                ref = refs[4 * layer + at]
                block = 2 * (core ^ (at // 2)) + (odd ^ (at % 2))
                cols = pl.ds(pl.multiple_of(block * D, D), D)
                start = pack * rows
                g_one[layer, :, cols] = ref[start : start + rows, :].astype(F32)
                to = pl.ds(pl.multiple_of(block * rows, rows), rows)
                g_two[layer, to, :] = ref[start + rows : start + 2 * rows, :].astype(F32)

    args = [scal] + [message for _, group in feeds for message in group]
    return small_kernel(
        body, "finish_feeds",
        [shape_of((LAYERS, rows, FF), F32), shape_of((LAYERS, FF // shards, D), F32)],
        [], args, 1,
    )


def finish_rest(shards, replicas, masks, count, scal, groups, places, silu_at):
    rows = D // shards
    span = shards * count
    total = replicas * span
    wide = 6 * D

    def body(scal_ref, *refs):
        g_mod, g_bias, g_qkv, g_out = refs[4 * len(groups) : 4 * len(groups) + 4]
        d_all, s_all, turned, joined = refs[4 * len(groups) + 4 :]
        me, core, rep = scal_ref[0], scal_ref[1], scal_ref[3]
        odd = (rep // 2) % 2
        for at in range(4):
            for j, mask in enumerate(masks):
                there = rep ^ (mask + 2 * (at % 2) + at // 2)
                to = pl.ds(pl.multiple_of(there * span, span), span)
                for (layer, half), (g, first) in places.items():
                    packs, parts, _ = groups[g]
                    base = packs * rows + (j * parts + first) * span
                    for b in range(3):
                        start = layer * wide + (half * 3 + b) * D
                        d_all[to, start : start + D] = refs[4 * g + at][
                            base + b * span : base + (b + 1) * span, :
                        ]
                g, part = silu_at
                base = groups[g][0] * rows + (j * groups[g][1] + part) * span
                s_all[to, :] = refs[4 * g + at][base : base + span, :].astype(F32)
        for layer, g in enumerate((2, 1)):
            for at in range(4):
                block = 2 * (core ^ (at // 2)) + (odd ^ (at % 2))
                cols = pl.ds(pl.multiple_of(block * D, D), D)
                joined[:, cols] = refs[4 * g + at][:rows, :].astype(F32)
            g_qkv[layer] = joined[:, : 3 * D]
            g_out[layer] = joined[:, 3 * D :]
        turned[...] = s_all[...].T
        mine = turned[pl.ds(pl.multiple_of(me * rows, rows), rows), :].astype(BF16)
        for layer in range(LAYERS):
            cols = slice(layer * wide, (layer + 1) * wide)
            g_mod[layer] = dot_nn(mine, d_all[:, cols])
            g_bias[layer : layer + 1, :] = jnp.sum(
                d_all[:, cols].astype(F32), axis=0, keepdims=True
            )

    args = [scal] + [message for _, _, group in groups for message in group]
    return small_kernel(
        body, "finish_rest",
        [
            shape_of((LAYERS, rows, wide), F32),
            shape_of((LAYERS, wide), F32),
            shape_of((LAYERS, rows, 3 * D), F32),
            shape_of((LAYERS, rows, D), F32),
        ],
        [
            pltpu.VMEM((total, LAYERS * wide), BF16),
            pltpu.VMEM((total, D), F32),
            pltpu.VMEM((D, total), F32),
            pltpu.VMEM((rows, FF), F32),
        ],
        args, 1,
    )


def flip(array, axis, size, mask):
    return lax.ppermute(array, axis, [(i, i ^ mask) for i in range(size)])


def after(value, *others):
    return lax.optimization_barrier((value, others))[0]


def tied(*values):
    return lax.optimization_barrier(values)


def per_device(
    shards, replicas, latents, conditioning, w_mod, b_mod, w_qkv, w_out, w_fc1, w_fc2, cotangent,
    live_counts,
):
    count = latents.shape[0]
    group = math.gcd(count, 2)
    rows = D // shards
    me = lax.axis_index("shard").astype(jnp.int32)
    rep = lax.axis_index("replica").astype(jnp.int32)
    core = rep % 2
    scal = jnp.stack([me, core, live_counts[0], rep])

    def to_shards(arrays):
        return [flip(arrays[k], "shard", shards, k) for k in range(1, shards)]

    def other_core(array):
        return flip(array, "replica", replicas, 1)

    def pack(layer):
        attn = jnp.concatenate([w_qkv[layer], w_out[layer]], axis=-1)
        second = jnp.concatenate(
            [w_fc2[layer, q * rows : (q + 1) * rows] for q in range(FF // D)], axis=-1
        )
        return attn, w_fc1[layer], second

    def our_half(own):
        return lax.dynamic_slice_in_dim(own, core * HALF, HALF, axis=2)

    cond_pieces = [conditioning] + to_shards([conditioning] * shards)
    attn0, one0, two0 = pack(0)
    own_a, own_f, own_1 = attn0[None], jnp.stack([one0, two0]), jnp.stack(pack(1))
    ours_a, cond_pieces = tied(our_half(own_a), cond_pieces)
    near_a = to_shards([ours_a] * shards)
    parts = modulation_partials(shards, scal, cond_pieces, w_mod, b_mod)
    mods = [parts[0]] + to_shards(parts)
    ours_f, ours_1, ours_2 = after(
        (our_half(own_f), our_half(own_1[:1]), our_half(own_1[1:])), parts[0]
    )
    near_f = to_shards([ours_f] * shards)
    far_a = [other_core(piece) for piece in near_a]
    near_1 = to_shards([after(ours_1, near_a[0])] * shards)

    mod, w_attn, normed, qkv, mixed, lse, proj, x_mid = first_attention(
        shards, group, scal, latents, mods, own_a, near_a, far_a
    )
    x_mid, near_f, near_1 = tied(x_mid, near_f, near_1)
    near_2 = to_shards([after(ours_2, x_mid)] * shards)
    far_f = [other_core(piece) for piece in near_f]
    w1, w2, normed_mid, act, slope, lift, x_one = first_feed(
        shards, group, scal, mod, own_f, near_f, far_f, x_mid
    )
    x_one, near_2 = tied(x_one, near_2)
    far_2 = [other_core(piece) for piece in near_2]
    far_1 = [other_core(piece) for piece in near_1]
    (
        output, grad_mid_1, d_1f, keep_1f, send_1f, w_attn_1, normed_1, qkv_1, mixed_1, lse_1,
        proj_1,
    ) = last_layer(shards, group, scal, mod, own_1, near_1 + near_2, far_1 + far_2, x_one, cotangent)

    def over_shards(message):
        return [message[0]] + to_shards(message)

    def over_chips(message, mask):
        return flip(message, "replica", replicas, mask)

    chip_masks = []
    mask = replicas // 2
    while mask > 2:
        chip_masks.append(mask)
        mask //= 2
    masks = [0]
    for mask in chip_masks:
        masks = masks + [other ^ mask for other in masks]

    def sums(name, members, *messages):
        return shard_sums(shards, f"shard_{name}", count, members, scal, messages)

    arrived_1f = other_core(send_1f)
    grad, d_1a, keep_1a, send_1a = attention_back(
        shards, group, 1, scal, mod, w_attn_1, grad_mid_1, x_one, normed_1, qkv_1, mixed_1, lse_1,
        proj_1,
    )
    grad, d_1a, send_1a, arrived_1f = tied(grad, d_1a, send_1a, arrived_1f)
    msg_1f = start_messages(shards, "start_1f", keep_1f, arrived_1f, d_1f, conditioning)
    arrived_1a = other_core(send_1a)
    shards_1f = over_shards(msg_1f)
    grad_mid, d_0f, keep_0f, send_0f = first_feed_back(
        shards, group, scal, mod, w1, w2, after(grad, msg_1f[0]), x_mid, normed_mid, act, slope,
        lift,
    )
    grad_mid, d_0f, send_0f, shards_1f, arrived_1a = tied(
        grad_mid, d_0f, send_0f, shards_1f, arrived_1a
    )
    arrived_0f = other_core(send_0f)
    msg_1a = start_messages(shards, "start_1a", keep_1a, arrived_1a, d_1a, None)
    shards_1a = over_shards(msg_1a)
    half_1f, away_1f, mods_1f = sums("1f", ((2, 4),), shards_1f)
    pair_1f = over_chips(away_1f, 2)
    msg_0f = start_messages(
        shards, "start_0f", keep_0f, after(arrived_0f, half_1f, msg_1a[0]), d_0f, None
    )
    shards_0f = over_shards(msg_0f)
    latents_grad, d_0a, keep_0a, send_0a = attention_back(
        shards, group, 0, scal, mod, w_attn, after(grad_mid, half_1f, msg_1a[0], msg_0f[0]),
        latents, normed, qkv, mixed, lse, proj,
    )
    d_0a, send_0a, pair_1f, shards_1a, shards_0f = tied(
        d_0a, send_0a, pair_1f, shards_1a, shards_0f
    )
    arrived_0a = other_core(send_0a)
    half_b, away_b, mods_b = sums("b", ((1, 3), (2, 3)), shards_1a, shards_0f)
    pair_b = over_chips(away_b, 2)
    msg_0a = start_messages(shards, "start_0a", keep_0a, after(arrived_0a, half_b), d_0a, None)
    shards_0a = over_shards(msg_0a)
    one_1f = pair_sums("pair_1f", half_1f, after(pair_1f, msg_0a[0]), mods_1f)
    one_b = pair_sums("pair_b", half_b, after(pair_b, one_1f), mods_b)
    half_0a, away_0a, mods_0a = sums("0a", ((1, 3),), shards_0a)
    pair_0a = over_chips(away_0a, 2)
    one_0a = pair_sums("pair_0a", half_0a, pair_0a, mods_0a)

    def rest(name, packs, message):
        for mask in chip_masks:
            message = chip_sums(
                f"chip_{name}_{mask}", packs * rows, message, over_chips(message, mask)
            )
        paired = over_chips(message, 2)
        return message, paired, other_core(message), other_core(paired)

    full_1f = rest("1f", 2, one_1f)
    full_b = rest("b", 3, one_b)
    full_0a = rest("0a", 1, one_0a)

    places = {(1, 1): (0, 0), (1, 0): (1, 0), (0, 1): (1, 3), (0, 0): (2, 0)}
    silu_parts = silu_grad_parts(shards, count, w_mod, places, (mods_1f, mods_b, mods_0a))
    silu_back = jnp.stack([silu_parts[0]] + to_shards(silu_parts))
    order = me ^ jnp.arange(shards, dtype=jnp.int32)
    d_silu = jnp.moveaxis(silu_back[order], 0, 1).reshape(count, D)
    sig = jax.nn.sigmoid(conditioning)
    cond_grad = d_silu * (sig * (1.0 + conditioning * (1.0 - sig)))

    g_one, g_two = finish_feeds(shards, scal, ((1, full_b), (0, full_1f)))
    g_mod, g_bias, g_qkv, g_out = finish_rest(
        shards, replicas, masks, count, scal,
        ((2, 4, full_1f), (3, 6, full_b), (1, 3, full_0a)), places, (0, 3),
    )
    width = 6 * D // shards
    g_bias = lax.dynamic_slice_in_dim(g_bias, me * width, width, axis=1)
    return output, latents_grad, cond_grad, g_mod, g_bias, g_qkv, g_out, g_one, g_two


def solution(mesh):
    slots = ("shard", "replica")
    in_specs = (
        P(slots, None, None),
        P(slots, None),
        P(None, "shard", None),
        P(None, "shard"),
        P(None, "shard", None),
        P(None, "shard", None),
        P(None, "shard", None),
        P(None, "shard", None),
        P(slots, None, None),
        P(slots),
    )
    out_specs = (
        P(slots, None, None),
        P(slots, None, None),
        P(slots, None),
        P(None, "shard", None),
        P(None, "shard"),
        P(None, "shard", None),
        P(None, "shard", None),
        P(None, "shard", None),
        P(None, "shard", None),
    )
    body = functools.partial(per_device, mesh.shape["shard"], mesh.shape["replica"])
    return jax.shard_map(body, mesh=mesh, in_specs=in_specs, out_specs=out_specs, check_vma=False)
```

```python
import functools
import math

import jax
import jax.numpy as jnp
from jax import lax
from jax.experimental import pallas as pl
from jax.experimental.pallas import tpu as pltpu
from jax.sharding import PartitionSpec as P

D = 384
HEADS = 6
HD = 64
FF = 1536
SEQ = 256
LAYERS = 2
EPS = 1e-06
SCALE = HD**-0.5
HALF = FF // 2

F32 = jnp.float32
BF16 = jnp.bfloat16
VMEM_LIMIT = 16 * 1024 * 1024
VMEM_MIB = {
    "attention_0": 16, "feed_0": 24, "layer_1": 36, "feed_back_0": 32, "attention_back_0": 24,
    "attention_back_1": 24,
}


def dot_nn(left, right):
    return jnp.dot(left, right, preferred_element_type=F32)


def dot_nt(left, right):
    return lax.dot_general(left, right, (((1,), (1,)), ((), ())), preferred_element_type=F32)


def as_columns(row):
    half = jnp.broadcast_to(row, (128, D)).T
    return jnp.concatenate([half, half], axis=1)


def token_sum(values):
    folded = values[:, :128] + values[:, 128:]
    return jnp.sum(folded.T, axis=0, keepdims=True)


def layer_norm(values):
    centered = values - jnp.mean(values, axis=0, keepdims=True)
    variance = jnp.mean(centered * centered, axis=0, keepdims=True)
    rstd = lax.rsqrt(variance + EPS)
    return centered * rstd, rstd


def layer_norm_pull(d_out, normal, rstd, scale_col):
    d_normal = d_out * (1.0 + scale_col)
    first = jnp.mean(d_normal, axis=0, keepdims=True)
    second = jnp.mean(d_normal * normal, axis=0, keepdims=True)
    return rstd * (d_normal - first - normal * second)


def lanes(index):
    return pl.ds(pl.multiple_of(index * SEQ, SEQ), SEQ)


def mod_row(mod_ref, latent, layer, part):
    start = layer * 6 * D + part * D
    return mod_ref[pl.ds(latent, 1), start : start + D]


def attend_forward(group, x_of, mod_ref, first, layer, w_t, normed, qkv, mixed, lse, proj, x_mid):
    for i in range(group):
        normal, _ = layer_norm(x_of(i))
        shift = as_columns(mod_row(mod_ref, first + i, layer, 0))
        scale = as_columns(mod_row(mod_ref, first + i, layer, 1))
        normed[:, i * SEQ : (i + 1) * SEQ] = (normal * (1.0 + scale) + shift).astype(BF16)
    for part in range(3):
        rows = slice(part * D, (part + 1) * D)
        packed = dot_nn(w_t[rows, :], normed[...])
        if part == 0:
            qkv[rows, :] = packed.astype(BF16) * jnp.asarray(SCALE, BF16)
        else:
            qkv[rows, :] = packed.astype(BF16)

    def head_step(step, carry):
        cols = lanes(step // (HEADS // 2))
        pair = step % (HEADS // 2)
        for side in range(2):
            head = pair * 2 + side
            row = pl.multiple_of(head * HD, HD)
            q_t = qkv[pl.ds(row, HD), cols]
            k_t = qkv[pl.ds(row + D, HD), cols]
            v_t = qkv[pl.ds(row + 2 * D, HD), cols]
            scores = dot_nn(k_t.T, q_t)
            highest = jnp.max(scores, axis=0, keepdims=True)
            probs = jnp.exp(scores - highest)
            total = jnp.sum(probs, axis=0, keepdims=True)
            out = dot_nn(v_t, probs.astype(BF16)) * (1.0 / total)
            mixed[pl.ds(row, HD), cols] = out.astype(BF16)
            lse[pl.ds(head, 1), cols] = highest + jnp.log(total)
        return carry

    lax.fori_loop(0, group * (HEADS // 2), head_step, 0, unroll=HEADS)
    projected = dot_nn(w_t[3 * D :, :], mixed[...])
    proj[...] = projected.astype(BF16)
    for i in range(group):
        gate = as_columns(mod_row(mod_ref, first + i, layer, 2))
        cols = slice(i * SEQ, (i + 1) * SEQ)
        x_mid[:, cols] = x_of(i) + gate * projected[:, cols]


def feed_forward(group, mod_ref, first, layer, w1_t, w2_t, x_mid, normed_mid, act, slope, lift, x_out):
    for i in range(group):
        cols = slice(i * SEQ, (i + 1) * SEQ)
        normal, _ = layer_norm(x_mid[:, cols])
        shift = as_columns(mod_row(mod_ref, first + i, layer, 3))
        scale = as_columns(mod_row(mod_ref, first + i, layer, 4))
        normed_mid[:, cols] = (normal * (1.0 + scale) + shift).astype(BF16)
    chunk = 384

    def hidden_step(step, carry):
        rows = pl.ds(pl.multiple_of(step * chunk, chunk), chunk)
        hidden = dot_nn(w1_t[rows, :], normed_mid[...])
        root = math.sqrt(2.0 / math.pi)
        square = hidden * hidden
        bent = jnp.tanh(hidden * (root + (root * 0.044715) * square))
        half = 0.5 + 0.5 * bent
        act[rows, :] = (hidden * half).astype(BF16)
        inner = root + (3.0 * root * 0.044715) * square
        slope[rows, :] = (half + hidden * inner * (half * (1.0 - bent))).astype(BF16)
        return carry

    lax.fori_loop(0, FF // chunk, hidden_step, 0, unroll=True)
    lifted = dot_nn(w2_t[...], act[...])
    lift[...] = lifted.astype(BF16)
    for i in range(group):
        gate = as_columns(mod_row(mod_ref, first + i, layer, 5))
        cols = slice(i * SEQ, (i + 1) * SEQ)
        x_out[:, cols] = x_mid[:, cols] + gate * lifted[:, cols]


def feed_backward(
    group, mod_ref, first, layer, w1, w2, grad, x_mid, normed_mid, act, slope, lift,
    d_lift, d_hidden, g1, g2, d_mod, base, grad_mid,
):
    for i in range(group):
        cols = slice(i * SEQ, (i + 1) * SEQ)
        gate = as_columns(mod_row(mod_ref, first + i, layer, 5))
        grad_now = grad[:, cols]
        d_lift[:, cols] = (grad_now * gate).astype(BF16)
        d_mod[pl.ds(first + i, 1), base + 2 * D : base + 3 * D] = token_sum(
            grad_now * lift[:, cols].astype(F32)
        )
    chunk = 512

    def hidden_step(step, carry):
        rows = pl.ds(pl.multiple_of(step * chunk, chunk), chunk)
        d_act = dot_nn(w2[rows, :], d_lift[...])
        d_hid = (d_act * slope[rows, :].astype(F32)).astype(BF16)
        d_hidden[rows, :] = d_hid
        g2[rows, :] += dot_nt(act[rows, :], d_lift[...])
        g1[:, rows] += dot_nt(normed_mid[...], d_hid)
        return carry

    lax.fori_loop(0, FF // chunk, hidden_step, 0, unroll=True)
    d_normed = dot_nn(w1[...], d_hidden[...])
    for i in range(group):
        cols = slice(i * SEQ, (i + 1) * SEQ)
        d_now = d_normed[:, cols]
        normal, rstd = layer_norm(x_mid[:, cols])
        scale = as_columns(mod_row(mod_ref, first + i, layer, 4))
        row = pl.ds(first + i, 1)
        d_mod[row, base : base + D] = token_sum(d_now)
        d_mod[row, base + D : base + 2 * D] = token_sum(d_now * normal)
        grad_mid[:, cols] = grad[:, cols] + layer_norm_pull(d_now, normal, rstd, scale)


def attend_backward(
    group, x_of, mod_ref, first, layer, w_attn, grad_mid, normed, qkv, mixed, lse, proj,
    d_proj, d_mixed, d_qkv, g_attn, d_mod, base, emit,
):
    for i in range(group):
        cols = slice(i * SEQ, (i + 1) * SEQ)
        gate = as_columns(mod_row(mod_ref, first + i, layer, 2))
        grad_now = grad_mid[:, cols]
        d_proj[:, cols] = (grad_now * gate).astype(BF16)
        d_mod[pl.ds(first + i, 1), base + 2 * D : base + 3 * D] = token_sum(
            grad_now * proj[:, cols].astype(F32)
        )
    d_mixed[...] = dot_nn(w_attn[:, 3 * D :], d_proj[...]).astype(BF16)
    g_attn[:, 3 * D :] += dot_nt(mixed[...], d_proj[...])

    def head_step(step, carry):
        cols = lanes(step // (HEADS // 2))
        pair = step % (HEADS // 2)
        for side in range(2):
            head = pair * 2 + side
            row = pl.multiple_of(head * HD, HD)
            q_t = qkv[pl.ds(row, HD), cols]
            k_t = qkv[pl.ds(row + D, HD), cols]
            v_t = qkv[pl.ds(row + 2 * D, HD), cols]
            d_out = d_mixed[pl.ds(row, HD), cols]
            scores = dot_nn(k_t.T, q_t)
            probs = jnp.exp(scores - lse[pl.ds(head, 1), cols])
            d_probs = dot_nn(v_t.T, d_out)
            delta = jnp.sum(probs * d_probs, axis=0, keepdims=True)
            d_scores = (probs * (d_probs - delta)).astype(BF16)
            d_qkv[pl.ds(row, HD), cols] = (dot_nn(k_t, d_scores) * SCALE).astype(BF16)
            d_qkv[pl.ds(row + D, HD), cols] = dot_nt(q_t, d_scores).astype(BF16)
            d_qkv[pl.ds(row + 2 * D, HD), cols] = dot_nt(d_out, probs.astype(BF16)).astype(BF16)
        return carry

    lax.fori_loop(0, group * (HEADS // 2), head_step, 0, unroll=HEADS)
    for part in range(3):
        rows = slice(part * D, (part + 1) * D)
        g_attn[:, rows] += dot_nt(normed[...], d_qkv[rows, :])
    d_normed = dot_nn(w_attn[:, : 3 * D], d_qkv[...])
    for i in range(group):
        cols = slice(i * SEQ, (i + 1) * SEQ)
        d_now = d_normed[:, cols]
        normal, rstd = layer_norm(x_of(i))
        scale = as_columns(mod_row(mod_ref, first + i, layer, 1))
        row = pl.ds(first + i, 1)
        d_mod[row, base : base + D] = token_sum(d_now)
        d_mod[row, base + D : base + 2 * D] = token_sum(d_now * normal)
        emit(i, grad_mid[:, cols] + layer_norm_pull(d_now, normal, rstd, scale))


def place_rows(shards, me, core, own, near, far, pack, target):
    rows = D // shards
    target[pl.ds(pl.multiple_of(me * rows, rows), rows), :] = own[pack]
    for k in range(1, shards):
        at = pl.ds(pl.multiple_of((me ^ k) * rows, rows), rows)
        target[at, pl.ds(pl.multiple_of(core * HALF, HALF), HALF)] = near[k - 1][pack]
        target[at, pl.ds(pl.multiple_of((1 - core) * HALF, HALF), HALF)] = far[k - 1][pack]


def unfold_second(shards, packed, natural):
    rows = D // shards
    for s in range(shards):
        for q in range(FF // D):
            start = s * (FF // shards) + q * rows
            natural[start : start + rows, :] = packed[
                s * rows : (s + 1) * rows, q * D : (q + 1) * D
            ]


def emit_grads(shards, me, core, g_attn, g1, g2, keep, send):
    rows = D // shards
    packs = [array for array in (g_attn, g1) if array is not None]
    for k in range(shards):
        owner = me ^ k
        start = pl.multiple_of(owner * rows, rows)
        for target, side in ((keep, core), (send, 1 - core)):
            cols = pl.ds(pl.multiple_of(side * HALF, HALF), HALF)
            for at, array in enumerate(packs):
                target[k, at] = array[pl.ds(start, rows), cols].astype(BF16)
            if g2 is not None:
                for q in range(HALF // D):
                    begin = owner * (FF // shards) + (side * (HALF // D) + q) * rows
                    target[k, len(packs), :, q * D : (q + 1) * D] = g2[
                        pl.ds(pl.multiple_of(begin, rows), rows), :
                    ].astype(BF16)


def whole():
    return None


def filled(specs, arrays):
    return [
        pl.BlockSpec(
            array.shape, lambda *_, dims=array.ndim: (0,) * dims, pipeline_mode=pl.Buffered(1)
        )
        if spec is None
        else spec
        for spec, array in zip(specs, arrays, strict=True)
    ]


def scalars():
    return pl.BlockSpec(memory_space=pltpu.SMEM)


def by_step(rows, group):
    return pl.BlockSpec((rows, group * SEQ), lambda step: (0, step))


def by_latent(group):
    return pl.BlockSpec((group, SEQ, D), lambda step: (step, 0, 0))


def shape_of(shape, dtype):
    return jax.ShapeDtypeStruct(shape, dtype)


def cost(flops, nbytes):
    return pl.CostEstimate(flops=int(flops), bytes_accessed=int(nbytes), transcendentals=0)


def run_kernel(body, name, steps, in_specs, out_specs, out_shape, scratch, flops, args):
    return pl.pallas_call(
        body,
        name=name,
        grid=(steps,),
        in_specs=filled(in_specs, args),
        out_specs=filled(out_specs, out_shape),
        out_shape=out_shape,
        scratch_shapes=scratch,
        cost_estimate=cost(8 * flops, 8 << 20),
        compiler_params=pltpu.CompilerParams(
            dimension_semantics=("arbitrary",), vmem_limit_bytes=VMEM_MIB[name] << 20
        ),
    )(*args)


def modulation_partials(shards, scal, cond_pieces, w_mod, b_mod):
    count = cond_pieces[0].shape[0]
    total = shards * count
    rows = D // shards
    wide = 6 * D

    def body(scal_ref, *refs):
        conds = refs[:shards]
        w_ref, b_ref = refs[shards : shards + 2]
        outs = refs[shards + 2 : 2 * shards + 2]
        table, turned = refs[2 * shards + 2 :]
        me = scal_ref[0]
        table[...] = jnp.zeros_like(table)
        for k in range(shards):
            table[k * count : (k + 1) * count, :] = conds[k][...]
        values = table[...]
        turned[...] = (values / (1.0 + jnp.exp(-values))).T
        mine = turned[pl.ds(pl.multiple_of(me * rows, rows), rows), :].T[:total, :].astype(BF16)
        owner = lax.broadcasted_iota(jnp.int32, (1, wide), 1) // (wide // shards)
        for layer in range(LAYERS):
            bias = jnp.concatenate([b_ref[layer : layer + 1, :].astype(F32)] * shards, axis=1)
            part = dot_nn(mine, w_ref[layer]) + jnp.where(owner == me, bias, 0.0)
            for k in range(shards):
                outs[k][:, layer * wide : (layer + 1) * wide] = part[k * count : (k + 1) * count, :]

    return small_kernel(
        body, "modulation_parts", [shape_of((count, LAYERS * wide), F32)] * shards,
        [pltpu.VMEM((128, D), F32), pltpu.VMEM((D, 128), F32)],
        (scal, *cond_pieces, w_mod, b_mod), 1,
    )


def first_attention(shards, group, scal, latents, mods, own, near, far):
    count = latents.shape[0]
    tokens = count * SEQ
    pieces = 2 * (shards - 1)

    def body(scal_ref, lat_ref, *refs):
        mod_refs = refs[:shards]
        own_ref = refs[shards]
        near_refs = refs[shards + 1 : shards + 1 + pieces // 2]
        far_refs = refs[shards + 1 + pieces // 2 : shards + 1 + pieces]
        mod, w_nat, normed, qkv, mixed, lse, proj, x_mid, w_t = refs[shards + 1 + pieces :]
        step = pl.program_id(0)

        @pl.when(step == 0)
        def _():
            total = mod_refs[0][...]
            for ref in mod_refs[1:]:
                total = total + ref[...]
            mod[...] = total
            place_rows(shards, scal_ref[0], scal_ref[1], own_ref, near_refs, far_refs, 0, w_nat)
            w_t[...] = w_nat[...].T

        def x_of(i):
            return lat_ref[i].astype(F32).T

        attend_forward(
            group, x_of, mod, step * group, 0, w_t, normed, qkv, mixed, lse, proj, x_mid
        )

    return run_kernel(
        body, "attention_0", count // group,
        [scalars(), by_latent(group)] + [whole()] * (shards + 1 + pieces),
        [whole(), whole()]
        + [by_step(r, group) for r in (D, 3 * D, D, HEADS, D, D)],
        [
            shape_of((count, LAYERS * 6 * D), F32),
            shape_of((D, FF), BF16),
            shape_of((D, tokens), BF16),
            shape_of((3 * D, tokens), BF16),
            shape_of((D, tokens), BF16),
            shape_of((HEADS, tokens), F32),
            shape_of((D, tokens), BF16),
            shape_of((D, tokens), F32),
        ],
        [pltpu.VMEM((FF, D), BF16)],
        2 * tokens * (4 * D * D + 2 * SEQ * D),
        (scal, latents, *mods, own, *near, *far),
    )


def first_feed(shards, group, scal, mod, own, near, far, x_mid):
    tokens = x_mid.shape[1]
    count = tokens // SEQ
    pieces = 2 * (shards - 1)

    def body(scal_ref, mod_ref, own_ref, *refs):
        near_refs = refs[: pieces // 2]
        far_refs = refs[pieces // 2 : pieces]
        x_mid_ref = refs[pieces]
        w1, w2, normed_mid, act, slope, lift, x_out, packed, w1_t, w2_t = refs[pieces + 1 :]
        step = pl.program_id(0)

        @pl.when(step == 0)
        def _():
            me, core = scal_ref[0], scal_ref[1]
            place_rows(shards, me, core, own_ref, near_refs, far_refs, 0, w1)
            place_rows(shards, me, core, own_ref, near_refs, far_refs, 1, packed)
            unfold_second(shards, packed, w2)
            w1_t[...] = w1[...].T
            w2_t[...] = w2[...].T

        feed_forward(
            group, mod_ref, step * group, 0, w1_t, w2_t, x_mid_ref, normed_mid, act, slope, lift,
            x_out,
        )

    return run_kernel(
        body, "feed_0", count // group,
        [scalars(), whole(), whole()] + [whole()] * pieces + [by_step(D, group)],
        [whole(), whole()] + [by_step(r, group) for r in (D, FF, FF, D, D)],
        [
            shape_of((D, FF), BF16),
            shape_of((FF, D), BF16),
            shape_of((D, tokens), BF16),
            shape_of((FF, tokens), BF16),
            shape_of((FF, tokens), BF16),
            shape_of((D, tokens), BF16),
            shape_of((D, tokens), F32),
        ],
        [pltpu.VMEM((D, FF), BF16), pltpu.VMEM((FF, D), BF16), pltpu.VMEM((D, FF), BF16)],
        4 * tokens * D * FF,
        (scal, mod, own, *near, *far, x_mid),
    )


def last_layer(shards, group, scal, mod, own, near, far, x_in, cotangent):
    tokens = x_in.shape[1]
    count = tokens // SEQ
    steps = count // group
    pieces = 4 * (shards - 1)
    layer = LAYERS - 1
    rows = D // shards
    wide = group * SEQ

    def body(scal_ref, mod_ref, own_ref, *refs):
        near_refs = refs[: pieces // 2]
        far_refs = refs[pieces // 2 : pieces]
        x_ref, cot_ref = refs[pieces : pieces + 2]
        (
            output, grad_mid, d_mod, keep, send, w_attn, normed, qkv, mixed, lse, proj,
        ) = refs[pieces + 2 : pieces + 13]
        (
            w1, w2, attn_t, w1_t, w2_t, x_mid, normed_mid, act, slope, lift, x_out, grad,
            d_lift, d_hidden, g1, g2,
        ) = refs[pieces + 13 :]
        step = pl.program_id(0)
        me, core, live = scal_ref[0], scal_ref[1], scal_ref[2]
        first = step * group

        @pl.when(step == 0)
        def _():
            near_1, near_2 = near_refs[: shards - 1], near_refs[shards - 1 :]
            far_1, far_2 = far_refs[: shards - 1], far_refs[shards - 1 :]
            place_rows(shards, me, core, own_ref.at[:1], near_1, far_1, 0, w_attn)
            place_rows(shards, me, core, own_ref.at[1:], near_2, far_2, 1, w1)
            unfold_second(shards, w1, w2)
            place_rows(shards, me, core, own_ref.at[1:], near_2, far_2, 0, w1)
            attn_t[...] = w_attn[...].T
            w1_t[...] = w1[...].T
            w2_t[...] = w2[...].T
            g1[...] = jnp.zeros_like(g1)
            g2[...] = jnp.zeros_like(g2)

        def x_of(i):
            return x_ref[:, i * SEQ : (i + 1) * SEQ]

        attend_forward(
            group, x_of, mod_ref, first, layer, attn_t, normed, qkv, mixed, lse, proj, x_mid
        )
        feed_forward(
            group, mod_ref, first, layer, w1_t, w2_t, x_mid, normed_mid, act, slope, lift, x_out
        )
        for i in range(group):
            cols = slice(i * SEQ, (i + 1) * SEQ)
            is_live = first + i < live
            output[i] = jnp.where(is_live, x_out[:, cols].T, 0.0).astype(BF16)
            grad[:, cols] = jnp.where(is_live, cot_ref[i].astype(F32).T, 0.0)
        feed_backward(
            group, mod_ref, first, layer, w1, w2, grad, x_mid, normed_mid, act, slope, lift,
            d_lift, d_hidden, g1, g2, d_mod, 0, grad_mid,
        )

        @pl.when(step == steps - 1)
        def _():
            emit_grads(shards, me, core, None, g1, g2, keep, send)

    def vm(rows, cols, dtype):
        return pltpu.VMEM((rows, cols), dtype)

    return run_kernel(
        body, "layer_1", steps,
        [scalars(), whole(), whole()] + [whole()] * pieces + [by_step(D, group), by_latent(group)],
        [by_latent(group), by_step(D, group), whole(), whole(), whole(), whole()]
        + [by_step(r, group) for r in (D, 3 * D, D, HEADS, D)],
        [
            shape_of((count, SEQ, D), BF16),
            shape_of((D, tokens), F32),
            shape_of((count, 3 * D), F32),
            shape_of((shards, 2, rows, HALF), BF16),
            shape_of((shards, 2, rows, HALF), BF16),
            shape_of((D, FF), BF16),
            shape_of((D, tokens), BF16),
            shape_of((3 * D, tokens), BF16),
            shape_of((D, tokens), BF16),
            shape_of((HEADS, tokens), F32),
            shape_of((D, tokens), BF16),
        ],
        [
            vm(D, FF, BF16), vm(FF, D, BF16), vm(FF, D, BF16), vm(FF, D, BF16), vm(D, FF, BF16),
            vm(D, wide, F32), vm(D, wide, BF16), vm(FF, wide, BF16), vm(FF, wide, BF16),
            vm(D, wide, BF16), vm(D, wide, F32), vm(D, wide, F32), vm(D, wide, BF16),
            vm(FF, wide, BF16), vm(D, FF, F32), vm(FF, D, F32),
        ],
        4 * tokens * (4 * D * D + 4 * D * FF + 2 * SEQ * D),
        (scal, mod, own, *near, *far, x_in, cotangent),
    )


def first_feed_back(shards, group, scal, mod, w1, w2, grad, x_mid, normed_mid, act, slope, lift):
    tokens = grad.shape[1]
    count = tokens // SEQ
    steps = count // group
    rows = D // shards
    wide = group * SEQ

    def body(
        scal_ref, mod_ref, w1_ref, w2_ref, grad_ref, x_ref, nm_ref, act_ref, slope_ref, lift_ref,
        grad_mid, d_mod, keep, send, d_lift, d_hidden, g1, g2,
    ):
        step = pl.program_id(0)

        @pl.when(step == 0)
        def _():
            g1[...] = jnp.zeros_like(g1)
            g2[...] = jnp.zeros_like(g2)

        feed_backward(
            group, mod_ref, step * group, 0, w1_ref, w2_ref, grad_ref, x_ref, nm_ref, act_ref,
            slope_ref, lift_ref, d_lift, d_hidden, g1, g2, d_mod, 0, grad_mid,
        )

        @pl.when(step == steps - 1)
        def _():
            emit_grads(shards, scal_ref[0], scal_ref[1], None, g1, g2, keep, send)

    return run_kernel(
        body, "feed_back_0", steps,
        [scalars(), whole(), whole(), whole()]
        + [by_step(r, group) for r in (D, D, D, FF, FF, D)],
        [by_step(D, group), whole(), whole(), whole()],
        [
            shape_of((D, tokens), F32),
            shape_of((count, 3 * D), F32),
            shape_of((shards, 2, rows, HALF), BF16),
            shape_of((shards, 2, rows, HALF), BF16),
        ],
        [
            pltpu.VMEM((D, wide), BF16), pltpu.VMEM((FF, wide), BF16),
            pltpu.VMEM((D, FF), F32), pltpu.VMEM((FF, D), F32),
        ],
        8 * tokens * D * FF,
        (scal, mod, w1, w2, grad, x_mid, normed_mid, act, slope, lift),
    )


def attention_back(
    shards, group, layer, scal, mod, w_attn, grad_mid, x_in, normed, qkv, mixed, lse, proj
):
    tokens = grad_mid.shape[1]
    count = tokens // SEQ
    steps = count // group
    rows = D // shards
    wide = group * SEQ

    def body(
        scal_ref, mod_ref, w_ref, grad_ref, x_ref, normed_ref, qkv_ref, mixed_ref, lse_ref,
        proj_ref, grad_out, d_mod, keep, send, d_proj, d_mixed, d_qkv, g_attn,
    ):
        step = pl.program_id(0)

        @pl.when(step == 0)
        def _():
            g_attn[...] = jnp.zeros_like(g_attn)

        def x_of(i):
            if layer == 0:
                return x_ref[i].astype(F32).T
            return x_ref[:, i * SEQ : (i + 1) * SEQ]

        def emit(i, values):
            if layer == 0:
                grad_out[i] = values.T.astype(BF16)
            else:
                grad_out[:, i * SEQ : (i + 1) * SEQ] = values

        attend_backward(
            group, x_of, mod_ref, step * group, layer, w_ref, grad_ref, normed_ref, qkv_ref,
            mixed_ref, lse_ref, proj_ref, d_proj, d_mixed, d_qkv, g_attn, d_mod, 0, emit,
        )

        @pl.when(step == steps - 1)
        def _():
            emit_grads(shards, scal_ref[0], scal_ref[1], g_attn, None, None, keep, send)

    io_spec = by_latent(group) if layer == 0 else by_step(D, group)
    out_form = shape_of((count, SEQ, D), BF16) if layer == 0 else shape_of((D, tokens), F32)
    return run_kernel(
        body, f"attention_back_{layer}", steps,
        [scalars(), whole(), whole(), by_step(D, group), io_spec]
        + [by_step(r, group) for r in (D, 3 * D, D, HEADS, D)],
        [io_spec, whole(), whole(), whole()],
        [
            out_form,
            shape_of((count, 3 * D), F32),
            shape_of((shards, 1, rows, HALF), BF16),
            shape_of((shards, 1, rows, HALF), BF16),
        ],
        [
            pltpu.VMEM((D, wide), BF16), pltpu.VMEM((D, wide), BF16),
            pltpu.VMEM((3 * D, wide), BF16), pltpu.VMEM((D, FF), F32),
        ],
        4 * tokens * (4 * D * D + 3 * SEQ * D),
        (scal, mod, w_attn, grad_mid, x_in, normed, qkv, mixed, lse, proj),
    )


BLOCKS = 2


def small_kernel(body, name, outs, scratch, args, smem=0, limit=VMEM_LIMIT):
    specs = [scalars()] * smem + [whole()] * (len(args) - smem)
    return pl.pallas_call(
        body,
        name=name,
        grid=(1,),
        in_specs=filled(specs, args),
        out_specs=filled([whole()] * len(outs), outs),
        out_shape=outs,
        scratch_shapes=scratch,
        cost_estimate=cost(1, 1),
        compiler_params=pltpu.CompilerParams(vmem_limit_bytes=limit),
    )(*args)


def silu(values):
    return values / (1.0 + jnp.exp(-values))


def start_messages(shards, name, keep, arrived, d_mod, conditioning):
    packs, rows = keep.shape[1:3]
    count = d_mod.shape[0]
    tail = BLOCKS * count
    tail = -(-tail // 16) * 16

    def body(keep_ref, arrived_ref, d_ref, *refs):
        cond_ref = refs[0] if conditioning is not None else None
        outs, table = refs[len(refs) - shards - 1 : -1], refs[-1]
        table[...] = jnp.zeros_like(table)
        table[:count, :] = d_ref[:, :HALF]
        table[count : 2 * count, : 3 * D - HALF] = d_ref[:, HALF:]
        if cond_ref is not None:
            table[count : 2 * count, 3 * D - HALF :] = silu(cond_ref[...])
        low = table[...].astype(BF16)
        for k in range(shards):
            for j in range(packs):
                total = keep_ref[k, j].astype(F32) + arrived_ref[k, j].astype(F32)
                outs[k][j * rows : (j + 1) * rows, :] = total.astype(BF16)
            outs[k][packs * rows :, :] = low

    args = (keep, arrived, d_mod) + (() if conditioning is None else (conditioning,))
    return small_kernel(
        body, name, [shape_of((packs * rows + tail, HALF), BF16)] * shards,
        [pltpu.VMEM((tail, HALF), F32)], args,
    )


def shard_sums(shards, name, count, members, scal, messages):
    rows = D // shards
    span = shards * count
    all_packs = sum(packs for packs, _ in members)
    all_parts = sum(parts for _, parts in members)

    def body(scal_ref, *refs):
        keep, send, joined, total, table = refs[shards * len(members) :]
        odd = (scal_ref[3] // 2) % 2
        first_pack, first_part = 0, 0
        for m, (packs, parts) in enumerate(members):
            ins = refs[shards * m : shards * (m + 1)]
            value = ins[0][: packs * rows, :].astype(F32)
            for k in range(1, shards):
                value = value + ins[k][: packs * rows, :].astype(F32)
            total[first_pack * rows : (first_pack + packs) * rows, :] = value
            for k in range(shards):
                extra = ins[k][packs * rows :, :].astype(F32)
                for b in range(parts):
                    at = (first_part + b) * span + k * count
                    first = (b // 2) * count
                    table[at : at + count, :] = extra[
                        first : first + count, (b % 2) * D : (b % 2 + 1) * D
                    ]
            first_pack += packs
            first_part += parts
        keep[...] = total[:, pl.ds(pl.multiple_of(odd * D, D), D)].astype(BF16)
        send[...] = total[:, pl.ds(pl.multiple_of((1 - odd) * D, D), D)].astype(BF16)
        joined[...] = table[...].astype(BF16)

    return small_kernel(
        body, name,
        [
            shape_of((all_packs * rows, D), BF16), shape_of((all_packs * rows, D), BF16),
            shape_of((all_parts * span, D), BF16),
        ],
        [pltpu.VMEM((all_packs * rows, HALF), F32), pltpu.VMEM((all_parts * span, D), F32)],
        (scal, *[message for phase in messages for message in phase]), 1,
    )


def pair_sums(name, keep, arrived, joined):
    size, extra = keep.shape[0], joined.shape[0]

    def body(a, b, c, out):
        out[:size, :] = (a[...].astype(F32) + b[...].astype(F32)).astype(BF16)
        out[size:, :] = c[...]

    return small_kernel(
        body, name, [shape_of((size + extra, D), BF16)], [], (keep, arrived, joined)
    )[0]


def chip_sums(name, size, ours, theirs):
    extra = ours.shape[0] - size

    def body(a, b, out):
        total = a[:size, :].astype(F32) + b[:size, :].astype(F32)
        out[:size, :] = total.astype(BF16)
        out[size : size + extra, :] = a[size:, :]
        out[size + extra :, :] = b[size:, :]

    return small_kernel(
        body, name, [shape_of((size + 2 * extra, D), BF16)], [], (ours, theirs)
    )[0]


def silu_grad_parts(shards, count, w_mod, places, joined):
    rows = D // shards
    span = shards * count

    def body(*refs):
        w_ref = refs[len(joined)]
        outs = refs[len(joined) + 1 :]
        total = None
        for (layer, half), (at, first) in places.items():
            for b in range(3):
                part = dot_nt(
                    refs[at][(first + b) * span : (first + b + 1) * span, :],
                    w_ref[layer, :, (3 * half + b) * D : (3 * half + b + 1) * D],
                )
                total = part if total is None else total + part
        for k in range(shards):
            outs[k][...] = total[k * count : (k + 1) * count, :]

    return small_kernel(
        body, "silu_grad_parts", [shape_of((count, rows), F32)] * shards, [], (*joined, w_mod),
    )


def finish_feeds(shards, scal, feeds):
    rows = D // shards

    def body(scal_ref, *refs):
        g_one, g_two = refs[4 * LAYERS :]
        core, odd = scal_ref[1], (scal_ref[3] // 2) % 2
        for layer, (pack, _) in enumerate(feeds):
            for at in range(4):
                ref = refs[4 * layer + at]
                block = 2 * (core ^ (at // 2)) + (odd ^ (at % 2))
                cols = pl.ds(pl.multiple_of(block * D, D), D)
                start = pack * rows
                g_one[layer, :, cols] = ref[start : start + rows, :].astype(F32)
                to = pl.ds(pl.multiple_of(block * rows, rows), rows)
                g_two[layer, to, :] = ref[start + rows : start + 2 * rows, :].astype(F32)

    args = [scal] + [message for _, group in feeds for message in group]
    return small_kernel(
        body, "finish_feeds",
        [shape_of((LAYERS, rows, FF), F32), shape_of((LAYERS, FF // shards, D), F32)],
        [], args, 1,
    )


def finish_rest(shards, replicas, masks, count, scal, groups, places, silu_at):
    rows = D // shards
    span = shards * count
    total = replicas * span
    wide = 6 * D

    def body(scal_ref, *refs):
        g_mod, g_bias, g_qkv, g_out = refs[4 * len(groups) : 4 * len(groups) + 4]
        d_all, s_all, turned, joined = refs[4 * len(groups) + 4 :]
        me, core, rep = scal_ref[0], scal_ref[1], scal_ref[3]
        odd = (rep // 2) % 2
        for at in range(4):
            for j, mask in enumerate(masks):
                there = rep ^ (mask + 2 * (at % 2) + at // 2)
                to = pl.ds(pl.multiple_of(there * span, span), span)
                for (layer, half), (g, first) in places.items():
                    packs, parts, _ = groups[g]
                    base = packs * rows + (j * parts + first) * span
                    for b in range(3):
                        start = layer * wide + (half * 3 + b) * D
                        d_all[to, start : start + D] = refs[4 * g + at][
                            base + b * span : base + (b + 1) * span, :
                        ]
                g, part = silu_at
                base = groups[g][0] * rows + (j * groups[g][1] + part) * span
                s_all[to, :] = refs[4 * g + at][base : base + span, :].astype(F32)
        for layer, g in enumerate((2, 1)):
            for at in range(4):
                block = 2 * (core ^ (at // 2)) + (odd ^ (at % 2))
                cols = pl.ds(pl.multiple_of(block * D, D), D)
                joined[:, cols] = refs[4 * g + at][:rows, :].astype(F32)
            g_qkv[layer] = joined[:, : 3 * D]
            g_out[layer] = joined[:, 3 * D :]
        turned[...] = s_all[...].T
        mine = turned[pl.ds(pl.multiple_of(me * rows, rows), rows), :].astype(BF16)
        for layer in range(LAYERS):
            cols = slice(layer * wide, (layer + 1) * wide)
            g_mod[layer] = dot_nn(mine, d_all[:, cols])
            g_bias[layer : layer + 1, :] = jnp.sum(
                d_all[:, cols].astype(F32), axis=0, keepdims=True
            )

    args = [scal] + [message for _, _, group in groups for message in group]
    return small_kernel(
        body, "finish_rest",
        [
            shape_of((LAYERS, rows, wide), F32),
            shape_of((LAYERS, wide), F32),
            shape_of((LAYERS, rows, 3 * D), F32),
            shape_of((LAYERS, rows, D), F32),
        ],
        [
            pltpu.VMEM((total, LAYERS * wide), BF16),
            pltpu.VMEM((total, D), F32),
            pltpu.VMEM((D, total), F32),
            pltpu.VMEM((rows, FF), F32),
        ],
        args, 1, VMEM_LIMIT if total <= 128 else 3 * VMEM_LIMIT + VMEM_LIMIT // 2,
    )


def flip(array, axis, size, mask):
    return lax.ppermute(array, axis, [(i, i ^ mask) for i in range(size)])


def after(value, *others):
    return lax.optimization_barrier((value, others))[0]


def tied(*values):
    return lax.optimization_barrier(values)


def per_device(
    shards, replicas, latents, conditioning, w_mod, b_mod, w_qkv, w_out, w_fc1, w_fc2, cotangent,
    live_counts,
):
    count = latents.shape[0]
    group = math.gcd(count, 2)
    rows = D // shards
    me = lax.axis_index("shard").astype(jnp.int32)
    rep = lax.axis_index("replica").astype(jnp.int32)
    core = rep % 2
    scal = jnp.stack([me, core, live_counts[0], rep])

    def to_shards(arrays):
        return [flip(arrays[k], "shard", shards, k) for k in range(1, shards)]

    def other_core(array):
        return flip(array, "replica", replicas, 1)

    def pack(layer):
        attn = jnp.concatenate([w_qkv[layer], w_out[layer]], axis=-1)
        second = jnp.concatenate(
            [w_fc2[layer, q * rows : (q + 1) * rows] for q in range(FF // D)], axis=-1
        )
        return attn, w_fc1[layer], second

    def our_half(own):
        return lax.dynamic_slice_in_dim(own, core * HALF, HALF, axis=2)

    cond_pieces = [conditioning] + to_shards([conditioning] * shards)
    attn0, one0, two0 = pack(0)
    own_a, own_f, own_1 = attn0[None], jnp.stack([one0, two0]), jnp.stack(pack(1))
    ours_a, cond_pieces = tied(our_half(own_a), cond_pieces)
    near_a = to_shards([ours_a] * shards)
    parts = modulation_partials(shards, scal, cond_pieces, w_mod, b_mod)
    mods = [parts[0]] + to_shards(parts)
    ours_f, ours_1, ours_2 = after(
        (our_half(own_f), our_half(own_1[:1]), our_half(own_1[1:])), parts[0]
    )
    near_f = to_shards([ours_f] * shards)
    far_a = [other_core(piece) for piece in near_a]
    near_1 = to_shards([after(ours_1, near_a[0])] * shards)

    mod, w_attn, normed, qkv, mixed, lse, proj, x_mid = first_attention(
        shards, group, scal, latents, mods, own_a, near_a, far_a
    )
    x_mid, near_f, near_1 = tied(x_mid, near_f, near_1)
    near_2 = to_shards([after(ours_2, x_mid)] * shards)
    far_f = [other_core(piece) for piece in near_f]
    w1, w2, normed_mid, act, slope, lift, x_one = first_feed(
        shards, group, scal, mod, own_f, near_f, far_f, x_mid
    )
    x_one, near_2 = tied(x_one, near_2)
    far_2 = [other_core(piece) for piece in near_2]
    far_1 = [other_core(piece) for piece in near_1]
    (
        output, grad_mid_1, d_1f, keep_1f, send_1f, w_attn_1, normed_1, qkv_1, mixed_1, lse_1,
        proj_1,
    ) = last_layer(shards, group, scal, mod, own_1, near_1 + near_2, far_1 + far_2, x_one, cotangent)

    def over_shards(message):
        return [message[0]] + to_shards(message)

    def over_chips(message, mask):
        return flip(message, "replica", replicas, mask)

    chip_masks = []
    mask = replicas // 2
    while mask > 2:
        chip_masks.append(mask)
        mask //= 2
    masks = [0]
    for mask in chip_masks:
        masks = masks + [other ^ mask for other in masks]

    def sums(name, members, *messages):
        return shard_sums(shards, f"shard_{name}", count, members, scal, messages)

    arrived_1f = other_core(send_1f)
    grad, d_1a, keep_1a, send_1a = attention_back(
        shards, group, 1, scal, mod, w_attn_1, grad_mid_1, x_one, normed_1, qkv_1, mixed_1, lse_1,
        proj_1,
    )
    grad, d_1a, send_1a, arrived_1f = tied(grad, d_1a, send_1a, arrived_1f)
    msg_1f = start_messages(shards, "start_1f", keep_1f, arrived_1f, d_1f, conditioning)
    arrived_1a = other_core(send_1a)
    shards_1f = over_shards(msg_1f)
    grad_mid, d_0f, keep_0f, send_0f = first_feed_back(
        shards, group, scal, mod, w1, w2, after(grad, msg_1f[0]), x_mid, normed_mid, act, slope,
        lift,
    )
    grad_mid, d_0f, send_0f, shards_1f, arrived_1a = tied(
        grad_mid, d_0f, send_0f, shards_1f, arrived_1a
    )
    arrived_0f = other_core(send_0f)
    msg_1a = start_messages(shards, "start_1a", keep_1a, arrived_1a, d_1a, None)
    shards_1a = over_shards(msg_1a)
    half_1f, away_1f, mods_1f = sums("1f", ((2, 4),), shards_1f)
    pair_1f = over_chips(away_1f, 2)
    msg_0f = start_messages(
        shards, "start_0f", keep_0f, after(arrived_0f, half_1f, msg_1a[0]), d_0f, None
    )
    shards_0f = over_shards(msg_0f)
    latents_grad, d_0a, keep_0a, send_0a = attention_back(
        shards, group, 0, scal, mod, w_attn, after(grad_mid, half_1f, msg_1a[0], msg_0f[0]),
        latents, normed, qkv, mixed, lse, proj,
    )
    d_0a, send_0a, pair_1f, shards_1a, shards_0f = tied(
        d_0a, send_0a, pair_1f, shards_1a, shards_0f
    )
    one_1f = pair_sums("pair_1f", half_1f, pair_1f, mods_1f)
    arrived_0a = other_core(after(send_0a, one_1f))
    msg_0a = start_messages(shards, "start_0a", keep_0a, arrived_0a, d_0a, None)
    shards_0a = over_shards(msg_0a)
    half_b, away_b, mods_b = sums(
        "b", ((1, 3), (2, 3)), after(shards_1a, one_1f, msg_0a), shards_0f
    )
    pair_b = over_chips(away_b, 2)
    got_1f = over_chips(one_1f, chip_masks[0])
    got_1f, pair_b, shards_0a = tied(got_1f, pair_b, shards_0a)

    def chips(name, packs, message, arrived):
        for mask in chip_masks:
            if mask != chip_masks[0]:
                arrived = over_chips(message, mask)
            message = chip_sums(f"chip_{name}_{mask}", packs * rows, message, arrived)
        return message

    def spread(message, paired):
        return message, paired, other_core(message), other_core(paired)

    one_b = pair_sums("pair_b", half_b, pair_b, mods_b)
    got_b = over_chips(one_b, chip_masks[0])
    half_0a, away_0a, mods_0a = sums("0a", ((1, 3),), after(shards_0a, one_b))
    pair_0a = over_chips(away_0a, 2)
    next_1f = chips("1f", 2, one_1f, got_1f)
    paired_1f = over_chips(next_1f, 2)
    one_0a = pair_sums("pair_0a", half_0a, pair_0a, mods_0a)
    got_0a = over_chips(one_0a, chip_masks[0])
    got_b, paired_1f, one_0a = tied(got_b, paired_1f, one_0a)
    next_b = chips("b", 3, one_b, got_b)
    next_0a = chips("0a", 1, one_0a, got_0a)
    full_1f = spread(next_1f, paired_1f)
    full_b = spread(next_b, over_chips(next_b, 2))
    full_0a = spread(next_0a, over_chips(next_0a, 2))

    places = {(1, 1): (0, 0), (1, 0): (1, 0), (0, 1): (1, 3), (0, 0): (2, 0)}
    silu_parts = silu_grad_parts(shards, count, w_mod, places, (mods_1f, mods_b, mods_0a))
    silu_back = jnp.stack([silu_parts[0]] + to_shards(silu_parts))
    order = me ^ jnp.arange(shards, dtype=jnp.int32)
    d_silu = jnp.moveaxis(silu_back[order], 0, 1).reshape(count, D)
    sig = jax.nn.sigmoid(conditioning)
    cond_grad = d_silu * (sig * (1.0 + conditioning * (1.0 - sig)))

    g_one, g_two = finish_feeds(shards, scal, ((1, full_b), (0, full_1f)))
    full_0a, g_one = tied(full_0a, g_one)
    g_mod, g_bias, g_qkv, g_out = finish_rest(
        shards, replicas, masks, count, scal,
        ((2, 4, full_1f), (3, 6, full_b), (1, 3, full_0a)), places, (0, 3),
    )
    width = 6 * D // shards
    g_bias = lax.dynamic_slice_in_dim(g_bias, me * width, width, axis=1)
    return output, latents_grad, cond_grad, g_mod, g_bias, g_qkv, g_out, g_one, g_two


def solution(mesh):
    slots = ("shard", "replica")
    in_specs = (
        P(slots, None, None),
        P(slots, None),
        P(None, "shard", None),
        P(None, "shard"),
        P(None, "shard", None),
        P(None, "shard", None),
        P(None, "shard", None),
        P(None, "shard", None),
        P(slots, None, None),
        P(slots),
    )
    out_specs = (
        P(slots, None, None),
        P(slots, None, None),
        P(slots, None),
        P(None, "shard", None),
        P(None, "shard"),
        P(None, "shard", None),
        P(None, "shard", None),
        P(None, "shard", None),
        P(None, "shard", None),
    )
    body = functools.partial(per_device, mesh.shape["shard"], mesh.shape["replica"])
    return jax.shard_map(body, mesh=mesh, in_specs=in_specs, out_specs=out_specs, check_vma=False)
```
